128 devices in a mesh: depth: 8 (over z, core), row: 16 (over y, x).
Axes of the slice: x: 4, y: 4, z: 4, core: 2. Of those that a mesh axis runs over, the one named last changes fastest.
Arguments:
- volume: float32 [384, 1024, 2048], P('depth', 'row'), may hold values from -6 to 6
- transfer: float32 [8], replicated, may hold values from 0.3 to 1.2
Outputs:
- image: float32 [4, 1024, 2048], P(None, 'row', 'depth')
The draws below stay inside these ranges and needn't reach their ends.
All inputs are finite; a program needn't handle non-finite values.
Results may differ from the reference program's by a relative error of at most 0.0003.
Values sent between devices are 32-bit elements; how exact they have to be, the bound alone decides.
A program may use at most 192 MiB of HBM per device.

```python
import jax
import jax.numpy as jnp
from jax import lax

X = 2048
CY = 64
NZ = 384
NY = 1024


def block_scale(rng, extent, cuts, least, high):
    gain, own = 1.0, jax.random.fold_in(rng, 6)
    for dim, blocks in cuts:
        draws = jnp.exp(jax.random.uniform(jax.random.fold_in(own, dim), (blocks,), jnp.float32, least / len(cuts), high / len(cuts)))
        gain = gain * jnp.repeat(draws, extent[dim] // blocks).reshape([-1 if axis == dim else 1 for axis in range(len(extent))])
    return gain


def bell_draw(key, shape, scale, bound, cuts=(), held_as=jnp.bfloat16):
    loudness = block_scale(key, shape, cuts, -0.22, 0.18) if cuts else 1.0
    drawn = jax.random.normal(key, shape, jnp.float32) * scale * loudness
    return jnp.minimum(jnp.maximum(drawn, -bound), bound).astype(held_as)


def setup_inputs(seed: int = 0) -> dict:
    keys = jax.random.split(jax.random.key(seed), 3)
    return {
        "volume": bell_draw(keys[0], (NZ, NY, X), 1.0, 6.0, ((0, 8), (1, 16)), jnp.float32),
        "transfer": jnp.clip(jax.random.uniform(keys[1], (8,), jnp.float32, 0.3, 1.2), 0.3, 1.2),
    }


def slope_cols(center):
    zero_col = jnp.zeros_like(center[..., :1])
    right = jnp.concatenate([center[..., 1:], zero_col], -1)
    left = jnp.concatenate([zero_col, center[..., :-1]], -1)
    return 0.5 * (right - left)

def emit(framed, transfer, slices):
    center = framed[1:-1, 1:-1, :]
    slope_depth = 0.5 * (framed[2:, 1:-1, :] - framed[:-2, 1:-1, :])
    slope_row = 0.5 * (framed[1:-1, 2:, :] - framed[1:-1, :-2, :])
    slope_col = slope_cols(center)
    inverse = lax.rsqrt(slope_depth * slope_depth + slope_row * slope_row + slope_col * slope_col + 1.0)
    lambert = jnp.abs((slope_depth + 2.0 * slope_row + 2.0 * slope_col) * inverse) / 3.0
    ambient = 0.5 * transfer[7]
    shading = ambient + (1.0 - ambient) * lambert
    depth_term = 2.0 * transfer[6] / slices * jax.nn.softplus(center)
    opacity = -jnp.expm1(-depth_term)
    tinting = jax.nn.sigmoid(2.0 * center)
    weight = shading * opacity
    emitted = jnp.stack([(transfer[channel] + transfer[3 + channel] * tinting) * weight for channel in range(3)])
    return (emitted, depth_term)

def reference(volume, transfer):
    blocks = NY // CY
    zero_slab = jnp.zeros((1, CY + 2, X), jnp.float32)

    def render(index):
        start = (index * CY).astype(jnp.int32)
        middle = lax.dynamic_slice_in_dim(volume, start, CY, 1)
        above = lax.dynamic_slice_in_dim(volume, jnp.maximum(start - 1, 0).astype(jnp.int32), 1, 1) * (index > 0).astype(jnp.float32)
        below = lax.dynamic_slice_in_dim(volume, jnp.minimum(start + CY, NY - 1).astype(jnp.int32), 1, 1) * (index < blocks - 1).astype(jnp.float32)
        framed = jnp.concatenate([above, middle, below], 1)
        framed = jnp.concatenate([zero_slab.astype(framed.dtype), framed, zero_slab.astype(framed.dtype)], 0)
        emitted, depth_term = emit(framed, transfer, NZ)
        before = jnp.cumsum(depth_term, 0) - depth_term
        color = lax.optimization_barrier(jnp.sum(jnp.exp(-before)[None] * emitted, 1))
        total = lax.optimization_barrier(jnp.sum(depth_term, 0))
        return jnp.concatenate([color, -jnp.expm1(-total)[None]], 0)
    pieces = lax.map(render, jnp.arange(blocks, dtype=jnp.int32))
    return jnp.transpose(pieces, (1, 0, 2, 3)).reshape(4, NY, X)
```

```python
import jax
import jax.numpy as jnp
from jax import lax
from jax.experimental import pallas as pl
from jax.experimental.pallas import tpu as pltpu
from jax.sharding import PartitionSpec as P

LOG2E = 1.4426950408889634
LN2 = 0.6931471805599453
LANES = 128
ROWS = 16
TOP = 8
MESH = pl.DeviceIdType.MESH


def block_of(depth, step):
    chip, core = depth // 2, depth % 2
    phase, half = step // 2, step % 2
    parity = core * half + (1 - core) * (1 - half)
    return 2 * ((chip + 1 + phase) % 4) + parity


def kernel(
    transfer,
    volume,
    image,
    vol,
    res,
    sib,
    parts,
    final,
    load_sem,
    halo_send,
    halo_recv,
    sib_send,
    sib_recv,
    part_send,
    part_recv,
    out_sem,
):
    depth, row = lax.axis_index("depth"), lax.axis_index("row")
    depths, rows = lax.axis_size("depth"), lax.axis_size("row")
    slices, height, _ = volume.shape
    chip, core = depth // 2, depth % 2
    sibling = depth + 1 - 2 * core
    first = 4 * ((chip + 1) % 4)

    def load(position):
        tile = (first + position) % 16
        return pltpu.make_async_copy(
            volume.at[:, :, pl.ds(pl.multiple_of(tile * LANES, LANES), LANES)],
            vol.at[tile + 1, pl.ds(1, slices), pl.ds(TOP, height), :],
            load_sem.at[tile],
        )

    lead = 2 - 2 * core
    order = [lead, lead + 1, lead + 15, lead + 2]
    second = [3 * core, 15 + 5 * core]
    for position in order + second:
        load(position).start()
    for position in range(5, 15):
        load(position).start()

    def partners(act):
        for offset in (2, 4, 6):
            act(True, {"depth": (depth + offset) % depths})
        act(depth > 0, {"depth": depth - 1})
        act(depth < depths - 1, {"depth": depth + 1})
        act(row > 0, {"row": row - 1})
        act(row < rows - 1, {"row": row + 1})

    barrier = pltpu.get_barrier_semaphore()

    def greet(there, device):
        def signal():
            pl.semaphore_signal(barrier, inc=1, device_id=device, device_id_type=MESH)

        signal() if there is True else pl.when(there)(signal)

    partners(greet)

    @pl.loop(0, slices)
    def _(z):
        vol[0, z + 1, pl.ds(TOP, height), :] = jnp.zeros((height, LANES), jnp.float32)
        vol[17, z + 1, pl.ds(TOP, height), :] = jnp.zeros((height, LANES), jnp.float32)

    def clear_slab(slab):
        @pl.loop(0, 16)
        def _(tile):
            vol[tile + 1, slab, pl.ds(TOP, height), :] = jnp.zeros((height, LANES), jnp.float32)

    def clear_row(at):
        @pl.loop(0, 16)
        def _(tile):
            @pl.loop(0, slices)
            def _(z):
                vol[tile + 1, z + 1, pl.ds(at, 1), :] = jnp.zeros((1, LANES), jnp.float32)

    pl.when(depth == 0)(lambda: clear_slab(0))
    pl.when(depth == depths - 1)(lambda: clear_slab(slices + 1))
    pl.when(row == 0)(lambda: clear_row(TOP - 1))
    pl.when(row == rows - 1)(lambda: clear_row(TOP + height))

    count = 3 + (depth > 0).astype(jnp.int32) + (depth < depths - 1).astype(jnp.int32)
    count = count + (row > 0).astype(jnp.int32) + (row < rows - 1).astype(jnp.int32)
    pl.semaphore_wait(barrier, count)

    def halo(kind, tile):
        columns = pl.ds(pl.multiple_of(tile * LANES, LANES), LANES)
        if kind < 2:
            source = volume.at[slices - 1 if kind == 0 else 0, :, columns]
            target = vol.at[tile + 1, 0 if kind == 0 else slices + 1, pl.ds(TOP, height), :]
            device = {"depth": depth + 1 if kind == 0 else depth - 1}
        else:
            source = volume.at[:, pl.ds(height - 1 if kind == 2 else 0, 1), columns]
            target = vol.at[
                tile + 1, pl.ds(1, slices), pl.ds(TOP - 1 if kind == 2 else TOP + height, 1), :
            ]
            device = {"row": row + 1 if kind == 2 else row - 1}
        return pltpu.make_async_remote_copy(
            src_ref=source,
            dst_ref=target,
            send_sem=halo_send.at[kind, tile],
            recv_sem=halo_recv.at[kind, tile],
            device_id=device,
            device_id_type=MESH,
        )

    can_send = (depth < depths - 1, depth > 0, row < rows - 1, row > 0)
    can_receive = (depth > 0, depth < depths - 1, row > 0, row < rows - 1)

    def send_halos(step):
        for kind, to in ((0, depth + 1), (1, depth - 1), (2, depth), (3, depth)):

            @pl.when(can_send[kind])
            def _(kind=kind, to=to):
                block = block_of(to, step)
                for side in range(2):
                    halo(kind, 2 * block + side).start()

    def receive_halos(kinds, block):
        for kind in kinds:

            @pl.when(can_receive[kind])
            def _(kind=kind):
                for side in range(2):
                    halo(kind, 2 * block + side).wait_recv()

    send_halos(0)
    send_halos(1)

    density = transfer[6] * (2.0 / (slices * depths))
    ambient = 0.5 * transfer[7]
    lift = 3.0 * ambient / (1.0 - ambient)
    lane = lax.broadcasted_iota(jnp.int32, (ROWS, LANES), 1)
    lowest, highest = lane == 0, lane == LANES - 1

    def march(tile, start, step):
        here = pl.ds(pl.multiple_of(TOP + start, 8), ROWS)
        above, below = pl.ds(TOP + start - 1, ROWS), pl.ds(TOP + start + 1, ROWS)

        def slab(z, carry):
            ahead, middle, logs, passing, white, tinted = carry
            behind = tuple(vol[tile + 1 + side, z + 2, here, :] for side in range(2))
            outer = (vol[tile, z + 1, here, :], vol[tile + 3, z + 1, here, :])
            lefts, rights = (outer[0], middle[0]), (middle[1], outer[1])
            out = []
            for side in range(2):
                value = middle[side]
                left = pltpu.roll(jnp.where(highest, lefts[side], value), 1, 1)
                right = pltpu.roll(jnp.where(lowest, rights[side], value), LANES - 1, 1)
                by_depth = behind[side] - ahead[side]
                by_row = vol[tile + 1 + side, z + 1, below, :] - vol[tile + 1 + side, z + 1, above, :]
                by_column = right - left
                plane = by_row + by_column
                along = by_depth + (plane + plane)
                square = (by_depth * by_depth + 4.0) + (by_row * by_row + by_column * by_column)
                lambert = jnp.abs(along) * lax.rsqrt(square)
                log = logs[side] - jnp.log2(1.0 + jnp.exp2(value * LOG2E))
                after = jnp.exp2(log * density)
                lit = (passing[side] - after) * (lambert + lift)
                out.append(
                    (log, after, white[side] + lit, tinted[side] + lit * jnp.tanh(value))
                )
            return (middle, behind) + tuple(zip(*out))

        zero = jnp.zeros((ROWS, LANES), jnp.float32)
        carry = tuple(
            tuple(vol[tile + 1 + side, z, here, :] for side in range(2)) for z in range(2)
        )
        carry = carry + ((zero,) * 2, (zero + 1.0,) * 2, (zero,) * 2, (zero,) * 2)
        _, _, logs, _, white, tinted = lax.fori_loop(0, slices, slab, carry, unroll=True)
        put = pl.ds(pl.multiple_of(start, 8), ROWS)
        for side in range(2):
            columns = pl.ds(side * LANES, LANES)
            res[step, 0, put, columns] = white[side]
            res[step, 1, put, columns] = tinted[side]
            res[step, 2, put, columns] = logs[side]

    def to_sibling(phase):
        return pltpu.make_async_remote_copy(
            src_ref=res.at[2 * phase],
            dst_ref=sib.at[phase],
            send_sem=sib_send.at[phase],
            recv_sem=sib_recv.at[phase],
            device_id={"depth": sibling},
            device_id_type=MESH,
        )

    def to_owner(phase):
        return pltpu.make_async_remote_copy(
            src_ref=res.at[2 * phase + 1],
            dst_ref=parts.at[phase],
            send_sem=part_send.at[phase],
            recv_sem=part_recv.at[phase],
            device_id={"depth": 2 * ((chip + 1 + phase) % 4) + core},
            device_id_type=MESH,
        )

    def join(phase):
        @pl.loop(0, height // ROWS)
        def _(chunk):
            at = pl.ds(pl.multiple_of(chunk * ROWS, ROWS), ROWS)
            mine = [res[2 * phase + 1, plane, at, :] for plane in range(3)]
            other = [sib[phase, plane, at, :] for plane in range(3)]
            front = [jnp.where(core == 0, a, b) for a, b in zip(mine, other)]
            back = [jnp.where(core == 0, b, a) for a, b in zip(mine, other)]
            through = jnp.exp2(front[2] * density)
            res[2 * phase + 1, 0, at, :] = front[0] + through * back[0]
            res[2 * phase + 1, 1, at, :] = front[1] + through * back[1]
            res[2 * phase + 1, 2, at, :] = front[2] + back[2]

    @pl.loop(0, 8)
    def _(step):
        block = block_of(depth, step)
        phase, half = step // 2, step % 2
        pl.when(step < 6)(lambda: send_halos(step + 2))

        @pl.when(step == 0)
        def _():
            for position in order:
                load(position).wait()

        @pl.when(step == 1)
        def _():
            for position in second:
                load(position).wait()

        @pl.when((half == 0) & (step >= 2) & (step < 6))
        def _():
            for position in range(1, 5):
                load(4 * phase + position).wait()

        @pl.when(step == 6)
        def _():
            for position in range(13, 15):
                load(position).wait()

        receive_halos((0, 1), block)

        @pl.loop(0, 2)
        def _(turn):
            pl.when(turn == 1)(lambda: receive_halos((2, 3), block))
            march(2 * block, ROWS * (1 - turn), step)
            march(2 * block, ROWS * (2 + turn), step)

        pl.when(half == 0)(lambda: to_sibling(phase).start())

        @pl.when(half == 1)
        def _():
            to_sibling(phase).wait_recv()
            join(phase)
            pl.when(phase < 3)(lambda: to_owner(phase).start())

    for phase in range(3):
        to_owner(phase).wait_recv()

    scale = (1.0 - ambient) / 3.0
    slope = [scale * 0.5 * transfer[3 + colour] for colour in range(3)]
    base = [scale * transfer[colour] + slope[colour] for colour in range(3)]

    @pl.loop(0, height // ROWS)
    def _(chunk):
        at = pl.ds(pl.multiple_of(chunk * ROWS, ROWS), ROWS)
        white = tinted = log = jnp.zeros((ROWS, 2 * LANES), jnp.float32)
        for front in range(4):
            phase = (chip + 3 - front) % 4
            own = phase == 3
            slot = phase % 3
            part = [
                jnp.where(own, res[7, plane, at, :], parts[slot, plane, at, :])
                for plane in range(3)
            ]
            through = jnp.exp2(log * density)
            white = white + through * part[0]
            tinted = tinted + through * part[1]
            log = log + part[2]
        for colour in range(3):
            final[colour, at, :] = base[colour] * white + slope[colour] * tinted
        bend = jnp.tanh(log * (density * (-0.5 * LN2)))
        final[3, at, :] = 2.0 * bend / (1.0 + bend)

    out = pltpu.make_async_copy(final, image, out_sem)
    out.start()
    for phase in range(4):
        to_sibling(phase).wait_send()
    for phase in range(3):
        to_owner(phase).wait_send()
    for kind in range(4):

        @pl.when(can_send[kind])
        def _(kind=kind):
            @pl.loop(0, 16)
            def _(tile):
                halo(kind, tile).wait_send()

    out.wait()


def on_device(volume, transfer):
    slices, height, columns = volume.shape
    own = columns // lax.axis_size("depth")
    f32 = jnp.float32
    dma = pltpu.SemaphoreType.DMA
    return pl.pallas_call(
        kernel,
        out_shape=jax.ShapeDtypeStruct((4, height, own), f32),
        in_specs=[
            pl.BlockSpec(memory_space=pltpu.SMEM),
            pl.BlockSpec(memory_space=pl.ANY),
        ],
        out_specs=pl.BlockSpec(memory_space=pl.ANY),
        scratch_shapes=[
            pltpu.VMEM((18, slices + 2, height + 16, LANES), f32),
            pltpu.VMEM((8, 3, height, own), f32),
            pltpu.VMEM((4, 3, height, own), f32),
            pltpu.VMEM((3, 3, height, own), f32),
            pltpu.VMEM((4, height, own), f32),
            dma((16,)),
            dma((4, 16)),
            dma((4, 16)),
            dma((4,)),
            dma((4,)),
            dma((3,)),
            dma((3,)),
            dma,
        ],
        compiler_params=pltpu.CompilerParams(
            collective_id=0, has_side_effects=True, vmem_limit_bytes=56 * 1024 * 1024
        ),
        name="render",
    )(transfer, volume)


def solution(mesh):
    in_specs = (P("depth", "row", None), P())
    out_specs = P(None, "row", "depth")
    return jax.shard_map(
        on_device, mesh=mesh, in_specs=in_specs, out_specs=out_specs, check_vma=False
    )
```

```python
import jax
import jax.numpy as jnp
from jax import lax
from jax.experimental import pallas as pl
from jax.experimental.pallas import tpu as pltpu
from jax.sharding import PartitionSpec as P

LOG2E = 1.4426950408889634
LN2 = 0.6931471805599453
LANES = 128
ROWS = 16
TOP = 8
EARLY = 5
MESH = pl.DeviceIdType.MESH


def block_of(depth, step):
    chip, core = depth // 2, depth % 2
    phase, half = step // 2, step % 2
    parity = core * half + (1 - core) * (1 - half)
    return 2 * ((chip + 1 + phase) % 4) + parity


def kernel(
    transfer,
    volume,
    image,
    vol,
    res,
    sib,
    parts,
    load_sem,
    halo_send,
    halo_recv,
    sib_send,
    sib_recv,
    part_send,
    part_recv,
):
    depth, row = lax.axis_index("depth"), lax.axis_index("row")
    depths, rows = lax.axis_size("depth"), lax.axis_size("row")
    slices, height, _ = volume.shape
    chip, core = depth // 2, depth % 2
    sibling = depth + 1 - 2 * core
    first = 4 * ((chip + 1) % 4)

    def load(position):
        tile = (first + position) % 16
        return pltpu.make_async_copy(
            volume.at[:, :, pl.ds(pl.multiple_of(tile * LANES, LANES), LANES)],
            vol.at[tile + 1, pl.ds(1, slices), pl.ds(TOP, height), :],
            load_sem.at[tile],
        )

    lead = 2 - 2 * core
    order = [lead, lead + 1, lead + 15, lead + 2]
    second = [3 * core, 15 + 5 * core]
    for position in order:
        load(position).start()

    def partners(act):
        for offset in (2, 4, 6):
            act(True, {"depth": (depth + offset) % depths})
        act(depth > 0, {"depth": depth - 1})
        act(depth < depths - 1, {"depth": depth + 1})
        act(row > 0, {"row": row - 1})
        act(row < rows - 1, {"row": row + 1})

    barrier = pltpu.get_barrier_semaphore()

    def greet(there, device):
        def signal():
            pl.semaphore_signal(barrier, inc=1, device_id=device, device_id_type=MESH)

        signal() if there is True else pl.when(there)(signal)

    partners(greet)

    @pl.loop(0, slices)
    def _(z):
        vol[0, z + 1, pl.ds(TOP, height), :] = jnp.zeros((height, LANES), jnp.float32)
        vol[17, z + 1, pl.ds(TOP, height), :] = jnp.zeros((height, LANES), jnp.float32)

    def clear_slab(slab):
        @pl.loop(0, 16)
        def _(tile):
            vol[tile + 1, slab, pl.ds(TOP, height), :] = jnp.zeros((height, LANES), jnp.float32)

    def clear_row(at):
        @pl.loop(0, 16)
        def _(tile):
            for z in range(slices):
                vol[tile + 1, z + 1, pl.ds(at, 1), :] = jnp.zeros((1, LANES), jnp.float32)

    pl.when(depth == 0)(lambda: clear_slab(0))
    pl.when(depth == depths - 1)(lambda: clear_slab(slices + 1))
    pl.when(row == 0)(lambda: clear_row(TOP - 1))
    pl.when(row == rows - 1)(lambda: clear_row(TOP + height))

    count = 3 + (depth > 0).astype(jnp.int32) + (depth < depths - 1).astype(jnp.int32)
    count = count + (row > 0).astype(jnp.int32) + (row < rows - 1).astype(jnp.int32)

    def halo(kind, tile):
        columns = pl.ds(pl.multiple_of(tile * LANES, LANES), LANES)
        if kind < 2:
            source = volume.at[slices - 1 if kind == 0 else 0, :, columns]
            target = vol.at[tile + 1, 0 if kind == 0 else slices + 1, pl.ds(TOP, height), :]
            device = {"depth": depth + 1 if kind == 0 else depth - 1}
        else:
            source = volume.at[:, pl.ds(height - 1 if kind == 2 else 0, 1), columns]
            target = vol.at[
                tile + 1, pl.ds(1, slices), pl.ds(TOP - 1 if kind == 2 else TOP + height, 1), :
            ]
            device = {"row": row + 1 if kind == 2 else row - 1}
        return pltpu.make_async_remote_copy(
            src_ref=source,
            dst_ref=target,
            send_sem=halo_send.at[kind],
            recv_sem=halo_recv.at[kind, tile // 2],
            device_id=device,
            device_id_type=MESH,
        )

    can_send = (depth < depths - 1, depth > 0, row < rows - 1, row > 0)
    can_receive = (depth > 0, depth < depths - 1, row > 0, row < rows - 1)

    def send_halos(step):
        for kind, to in ((0, depth + 1), (1, depth - 1), (2, depth), (3, depth)):

            @pl.when(can_send[kind])
            def _(kind=kind, to=to):
                block = block_of(to, step)
                for side in range(2):
                    halo(kind, 2 * block + side).start()

    def receive_halos(kinds, block):
        tiles = pl.ds(2 * block + 1, 2)
        landed = (
            vol.at[tiles, 0, pl.ds(TOP, height), :],
            vol.at[tiles, slices + 1, pl.ds(TOP, height), :],
            vol.at[tiles, pl.ds(1, slices), pl.ds(TOP - 1, 1), :],
            vol.at[tiles, pl.ds(1, slices), pl.ds(TOP + height, 1), :],
        )
        for kind in kinds:

            @pl.when(can_receive[kind])
            def _(kind=kind):
                both = landed[kind]
                pltpu.make_async_copy(both, both, halo_recv.at[kind, block]).wait()

    density = transfer[6] * (2.0 / (slices * depths))
    ambient = 0.5 * transfer[7]
    lift = 3.0 * ambient / (1.0 - ambient)
    lane = lax.broadcasted_iota(jnp.int32, (ROWS, LANES), 1)
    lowest, highest = lane == 0, lane == LANES - 1

    def shade(tile, z, here, above, below, ahead, middle, behind, side):
        value = middle[side]
        if side == 0:
            before, after = vol[tile, z + 1, here, :], middle[1]
        else:
            before, after = middle[0], vol[tile + 3, z + 1, here, :]
        left = pltpu.roll(jnp.where(highest, before, value), 1, 1)
        right = pltpu.roll(jnp.where(lowest, after, value), LANES - 1, 1)
        by_depth = behind - ahead
        by_row = vol[tile + 1 + side, z + 1, below, :] - vol[tile + 1 + side, z + 1, above, :]
        by_column = right - left
        plane = by_row + by_column
        along = by_depth + (plane + plane)
        square = (by_depth * by_depth + 4.0) + (by_row * by_row + by_column * by_column)
        return jnp.abs(along) * lax.rsqrt(square)

    def around(start):
        return tuple(pl.ds(TOP + start + shift, ROWS) for shift in (0, -1, 1))

    def march(tile, start, step, ends):
        here, above, below = around(start)

        def cells(slab):
            return tuple(vol[tile + 1 + side, slab, here, :] for side in range(2))

        def absorb(middle, side, log):
            log = log - jnp.log2(1.0 + jnp.exp2(middle[side] * LOG2E))
            return log, jnp.exp2(log * density)

        def slab(z, carry):
            ahead, middle, logs, passing, white, tinted = carry
            behind = cells(z + 2)
            out = []
            for side in range(2):
                lambert = shade(tile, z, here, above, below, ahead[side], middle, behind[side], side)
                log, after = absorb(middle, side, logs[side])
                lit = (passing[side] - after) * (lambert + lift)
                tint = jnp.tanh(middle[side])
                out.append((log, after, white[side] + lit, tinted[side] + lit * tint))
            return (middle, behind) + tuple(zip(*out))

        zero = jnp.zeros((ROWS, LANES), jnp.float32)
        if ends:
            carry = (cells(0), cells(1), (zero,) * 2, (zero + 1.0,) * 2, (zero,) * 2, (zero,) * 2)
            _, _, logs, _, white, tinted = lax.fori_loop(0, slices, slab, carry, unroll=True)
        else:
            middle = cells(1)
            logs, passing = zip(*(absorb(middle, side, zero) for side in range(2)))
            carry = (middle, cells(2), logs, passing, (zero,) * 2, (zero,) * 2)
            carry = lax.fori_loop(1, slices - 1, slab, carry, unroll=True)
            _, middle, logs, _, white, tinted = carry
            logs = tuple(absorb(middle, side, logs[side])[0] for side in range(2))
        put = pl.ds(pl.multiple_of(start, 8), ROWS)
        for side in range(2):
            columns = pl.ds(side * LANES, LANES)
            res[step, 0, put, columns] = white[side]
            res[step, 1, put, columns] = tinted[side]
            res[step, 2, put, columns] = logs[side]

    def add_ends(tile, start, step):
        here, above, below = around(start)
        put = pl.ds(pl.multiple_of(start, 8), ROWS)
        for z in (0, slices - 1):
            ahead, middle, behind = (
                tuple(vol[tile + 1 + side, z + shift, here, :] for side in range(2))
                for shift in range(3)
            )
            for side in range(2):
                columns = pl.ds(side * LANES, LANES)
                value = middle[side]
                lambert = shade(tile, z, here, above, below, ahead[side], middle, behind[side], side)
                own = jnp.log2(1.0 + jnp.exp2(value * LOG2E))
                if z == 0:
                    passed = 1.0 - jnp.exp2(own * -density)
                else:
                    log = res[step, 2, put, columns]
                    passed = jnp.exp2((log + own) * density) - jnp.exp2(log * density)
                lit = passed * (lambert + lift)
                res[step, 0, put, columns] += lit
                res[step, 1, put, columns] += lit * jnp.tanh(value)

    def to_sibling(phase):
        return pltpu.make_async_remote_copy(
            src_ref=res.at[2 * phase],
            dst_ref=sib.at[phase],
            send_sem=sib_send.at[phase],
            recv_sem=sib_recv.at[phase],
            device_id={"depth": sibling},
            device_id_type=MESH,
        )

    def to_owner(phase):
        return pltpu.make_async_remote_copy(
            src_ref=res.at[2 * phase + 1],
            dst_ref=parts.at[phase],
            send_sem=part_send.at[phase],
            recv_sem=part_recv.at[phase],
            device_id={"depth": 2 * ((chip + 1 + phase) % 4) + core},
            device_id_type=MESH,
        )

    def join(phase):
        @pl.loop(0, height // ROWS)
        def _(chunk):
            at = pl.ds(pl.multiple_of(chunk * ROWS, ROWS), ROWS)
            mine = [res[2 * phase + 1, plane, at, :] for plane in range(3)]
            other = [sib[phase, plane, at, :] for plane in range(3)]
            front = [jnp.where(core == 0, a, b) for a, b in zip(mine, other)]
            back = [jnp.where(core == 0, b, a) for a, b in zip(mine, other)]
            through = jnp.exp2(front[2] * density)
            res[2 * phase + 1, 0, at, :] = front[0] + through * back[0]
            res[2 * phase + 1, 1, at, :] = front[1] + through * back[1]
            res[2 * phase + 1, 2, at, :] = front[2] + back[2]

    def wait_loads(step):
        @pl.when(step == 0)
        def _():
            for position in order:
                load(position).wait()
            for position in second:
                load(position).start()
            for position in range(5, 15):
                load(position).start()

        @pl.when(step == 1)
        def _():
            for position in second:
                load(position).wait()

        @pl.when((step == 2) | (step == 4))
        def _():
            for position in range(1, 5):
                load(2 * step + position).wait()

        @pl.when(step == 6)
        def _():
            for position in range(13, 15):
                load(position).wait()

    @pl.loop(0, EARLY)
    def _(step):
        wait_loads(step)

        @pl.when(step == 1)
        def _():
            pl.semaphore_wait(barrier, count)

        @pl.when(step > 0)
        def _():
            send_halos(2 * step - 2)
            send_halos(2 * step - 1)

        block = block_of(depth, step)
        march(2 * block, ROWS, step, False)
        march(2 * block, 2 * ROWS, step, False)

    @pl.loop(0, 16 - EARLY)
    def _(index):
        late = jnp.maximum(index - EARLY, 0)
        step = jnp.where(index < EARLY, index, EARLY + late // 2)
        turn = jnp.where(index < EARLY, 1, late % 2)
        phase, half = step // 2, step % 2
        block = block_of(depth, step)

        @pl.when(turn == 0)
        def _():
            wait_loads(step)
            receive_halos((0, 1), block)

        @pl.when(index < EARLY)
        def _():
            receive_halos((0, 1), block)
            add_ends(2 * block, ROWS, step)
            add_ends(2 * block, 2 * ROWS, step)

        pl.when(turn == 1)(lambda: receive_halos((2, 3), block))
        march(2 * block, ROWS * (1 - turn), step, True)
        march(2 * block, ROWS * (2 + turn), step, True)

        pl.when((turn == 1) & (half == 0))(lambda: to_sibling(phase).start())

        @pl.when((turn == 1) & (half == 1))
        def _():
            to_sibling(phase).wait_recv()
            join(phase)
            pl.when(phase < 3)(lambda: to_owner(phase).start())

    for phase in range(3):
        to_owner(phase).wait_recv()

    scale = (1.0 - ambient) / 3.0
    slope = [scale * 0.5 * transfer[3 + colour] for colour in range(3)]
    base = [scale * transfer[colour] + slope[colour] for colour in range(3)]

    @pl.loop(0, height // ROWS)
    def _(chunk):
        at = pl.ds(pl.multiple_of(chunk * ROWS, ROWS), ROWS)
        white = tinted = log = jnp.zeros((ROWS, 2 * LANES), jnp.float32)
        for front in range(4):
            phase = (chip + 3 - front) % 4
            own = phase == 3
            slot = phase % 3
            part = [
                jnp.where(own, res[7, plane, at, :], parts[slot, plane, at, :])
                for plane in range(3)
            ]
            through = jnp.exp2(log * density)
            white = white + through * part[0]
            tinted = tinted + through * part[1]
            log = log + part[2]
        for colour in range(3):
            image[colour, at, :] = base[colour] * white + slope[colour] * tinted
        bend = jnp.tanh(log * (density * (-0.5 * LN2)))
        image[3, at, :] = 2.0 * bend / (1.0 + bend)

    for phase in range(4):
        to_sibling(phase).wait_send()
    for phase in range(3):
        to_owner(phase).wait_send()
    for kind in range(4):

        @pl.when(can_send[kind])
        def _(kind=kind):
            sent = volume.at[0] if kind < 2 else volume.at[:, pl.ds(0, 1), :]
            pltpu.make_async_copy(sent, sent, halo_send.at[kind]).wait()


def on_device(volume, transfer):
    slices, height, columns = volume.shape
    own = columns // lax.axis_size("depth")
    f32 = jnp.float32
    dma = pltpu.SemaphoreType.DMA
    return pl.pallas_call(
        kernel,
        out_shape=pltpu.VMEM((4, height, own), f32),
        in_specs=[
            pl.BlockSpec(memory_space=pltpu.SMEM),
            pl.BlockSpec(memory_space=pl.ANY),
        ],
        out_specs=pl.BlockSpec(memory_space=pltpu.VMEM),
        scratch_shapes=[
            pltpu.VMEM((18, slices + 2, height + 16, LANES), f32),
            pltpu.VMEM((8, 3, height, own), f32),
            pltpu.VMEM((4, 3, height, own), f32),
            pltpu.VMEM((3, 3, height, own), f32),
            dma((16,)),
            dma((4,)),
            dma((4, 8)),
            dma((4,)),
            dma((4,)),
            dma((3,)),
            dma((3,)),
        ],
        compiler_params=pltpu.CompilerParams(
            collective_id=0, has_side_effects=True, vmem_limit_bytes=56 * 1024 * 1024
        ),
        name="render",
    )(transfer, volume)


def solution(mesh):
    in_specs = (P("depth", "row", None), P())
    out_specs = P(None, "row", "depth")
    return jax.shard_map(
        on_device, mesh=mesh, in_specs=in_specs, out_specs=out_specs, check_vma=False
    )
```

```python
import jax
import jax.numpy as jnp
from jax import lax
from jax.experimental import pallas as pl
from jax.experimental.pallas import tpu as pltpu
from jax.sharding import PartitionSpec as P

LOG2E = 1.4426950408889634
LN2 = 0.6931471805599453
LANES = 128
ROWS = 16
TOP = 8
EARLY = 5
MESH = pl.DeviceIdType.MESH


def ahead_of(phase):
    return jnp.where(phase == 0, 2, jnp.where(phase == 1, 1, jnp.where(phase == 2, 3, 0)))


def block_of(depth, step):
    chip, core = depth // 2, depth % 2
    phase, half = step // 2, step % 2
    parity = core * half + (1 - core) * (1 - half)
    return 2 * ((chip + ahead_of(phase)) % 4) + parity


def kernel(
    transfer,
    volume,
    image,
    vol,
    slabs,
    res,
    sib,
    parts,
    load_sem,
    halo_send,
    halo_recv,
    sib_send,
    sib_recv,
    part_send,
    part_recv,
):
    depth, row = lax.axis_index("depth"), lax.axis_index("row")
    depths, rows = lax.axis_size("depth"), lax.axis_size("row")
    slices, height, _ = volume.shape
    chip, core = depth // 2, depth % 2
    sibling = depth + 1 - 2 * core
    first = 4 * ((chip + 2) % 4)

    def load(position):
        tile = (first + position) % 16
        return pltpu.make_async_copy(
            volume.at[:, :, pl.ds(pl.multiple_of(tile * LANES, LANES), LANES)],
            vol.at[tile + 1, pl.ds(1, slices), pl.ds(TOP, height), :],
            load_sem.at[tile],
        )

    lead = 2 - 2 * core
    order = [lead, lead + 1, lead + 15, lead + 2]
    second = [3 * core, 15 + 5 * core]
    for position in order + second:
        load(position).start()

    def partners(act):
        for offset in (2, 4, 6):
            act(True, {"depth": (depth + offset) % depths})
        act(depth > 0, {"depth": depth - 1})
        act(depth < depths - 1, {"depth": depth + 1})
        act(row > 0, {"row": row - 1})
        act(row < rows - 1, {"row": row + 1})

    barrier = pltpu.get_barrier_semaphore()

    def greet(there, device):
        def signal():
            pl.semaphore_signal(barrier, inc=1, device_id=device, device_id_type=MESH)

        signal() if there is True else pl.when(there)(signal)

    partners(greet)

    @pl.loop(0, slices)
    def _(z):
        vol[0, z + 1, pl.ds(TOP, height), :] = jnp.zeros((height, LANES), jnp.float32)
        vol[17, z + 1, pl.ds(TOP, height), :] = jnp.zeros((height, LANES), jnp.float32)

    def clear_slab(kind):
        slabs[kind] = jnp.zeros((height, 16 * LANES), jnp.float32)

    def clear_row(at):
        @pl.loop(0, 16)
        def _(tile):
            for z in range(slices):
                vol[tile + 1, z + 1, pl.ds(at, 1), :] = jnp.zeros((1, LANES), jnp.float32)

    pl.when(depth == 0)(lambda: clear_slab(0))
    pl.when(depth == depths - 1)(lambda: clear_slab(1))
    pl.when(row == 0)(lambda: clear_row(TOP - 1))
    pl.when(row == rows - 1)(lambda: clear_row(TOP + height))

    count = 3 + (depth > 0).astype(jnp.int32) + (depth < depths - 1).astype(jnp.int32)
    count = count + (row > 0).astype(jnp.int32) + (row < rows - 1).astype(jnp.int32)

    def halo(kind, group):
        if kind < 2:
            columns = pl.ds(pl.multiple_of(group * 4 * LANES, 4 * LANES), 4 * LANES)
            source = volume.at[slices - 1 if kind == 0 else 0, :, columns]
            target = slabs.at[kind, :, columns]
            device = {"depth": depth + 1 if kind == 0 else depth - 1}
        else:
            tiles = pl.ds(4 * group + 1, 4)
            last, beyond = (TOP + height - 1, TOP - 1) if kind == 2 else (TOP, TOP + height)
            source = vol.at[tiles, pl.ds(1, slices), pl.ds(last, 1), :]
            target = vol.at[tiles, pl.ds(1, slices), pl.ds(beyond, 1), :]
            device = {"row": row + 1 if kind == 2 else row - 1}
        return pltpu.make_async_remote_copy(
            src_ref=source,
            dst_ref=target,
            send_sem=halo_send.at[kind],
            recv_sem=halo_recv.at[kind, group],
            device_id=device,
            device_id_type=MESH,
        )

    can_send = (depth < depths - 1, depth > 0, row < rows - 1, row > 0)
    can_receive = (depth > 0, depth < depths - 1, row > 0, row < rows - 1)

    def group_of(depth, phase):
        return (depth // 2 + ahead_of(phase)) % 4

    def send_halos(kinds, phase):
        for kind in kinds:

            @pl.when(can_send[kind])
            def _(kind=kind):
                halo(kind, group_of((depth + 1, depth - 1, depth, depth)[kind], phase)).start()

    def receive_halos(kinds, phase):
        for kind in kinds:

            @pl.when(can_receive[kind])
            def _(kind=kind):
                halo(kind, group_of(depth, phase)).wait_recv()

    density = transfer[6] * (2.0 / (slices * depths))
    ambient = 0.5 * transfer[7]
    lift = 3.0 * ambient / (1.0 - ambient)
    lane = lax.broadcasted_iota(jnp.int32, (ROWS, LANES), 1)
    lowest, highest = lane == 0, lane == LANES - 1

    def shade(tile, z, here, above, below, ahead, middle, behind, side):
        value = middle[side]
        if side == 0:
            before, after = vol[tile, z + 1, here, :], middle[1]
        else:
            before, after = middle[0], vol[tile + 3, z + 1, here, :]
        left = pltpu.roll(jnp.where(highest, before, value), 1, 1)
        right = pltpu.roll(jnp.where(lowest, after, value), LANES - 1, 1)
        by_depth = behind - ahead
        by_row = vol[tile + 1 + side, z + 1, below, :] - vol[tile + 1 + side, z + 1, above, :]
        by_column = right - left
        plane = by_row + by_column
        along = by_depth + (plane + plane)
        square = (by_depth * by_depth + 4.0) + (by_row * by_row + by_column * by_column)
        return jnp.abs(along) * lax.rsqrt(square)

    def around(start):
        return tuple(pl.ds(TOP + start + shift, ROWS) for shift in (0, -1, 1))

    def outside(tile, start):
        put = pl.ds(pl.multiple_of(start, 8), ROWS)
        columns = [pl.ds(pl.multiple_of((tile + side) * LANES, LANES), LANES) for side in range(2)]
        return [lambda kind=kind: tuple(slabs[kind, put, column] for column in columns) for kind in range(2)]

    def march(tile, start, step, ends):
        here, above, below = around(start)

        def cells(slab):
            return tuple(vol[tile + 1 + side, slab, here, :] for side in range(2))

        first, last = outside(tile, start)

        def absorb(middle, side, log):
            log = log - jnp.log2(1.0 + jnp.exp2(middle[side] * LOG2E))
            return log, jnp.exp2(log * density)

        def slab(z, carry, behind=None):
            ahead, middle, logs, passing, white, tinted = carry
            behind = cells(z + 2) if behind is None else behind
            out = []
            for side in range(2):
                lambert = shade(tile, z, here, above, below, ahead[side], middle, behind[side], side)
                log, after = absorb(middle, side, logs[side])
                lit = (passing[side] - after) * (lambert + lift)
                tint = jnp.tanh(middle[side])
                out.append((log, after, white[side] + lit, tinted[side] + lit * tint))
            return (middle, behind) + tuple(zip(*out))

        zero = jnp.zeros((ROWS, LANES), jnp.float32)
        if ends:
            carry = (first(), cells(1), (zero,) * 2, (zero + 1.0,) * 2, (zero,) * 2, (zero,) * 2)
            carry = lax.fori_loop(0, slices - 1, slab, carry, unroll=True)
            _, _, logs, _, white, tinted = slab(slices - 1, carry, last())
        else:
            middle = cells(1)
            logs, passing = zip(*(absorb(middle, side, zero) for side in range(2)))
            carry = (middle, cells(2), logs, passing, (zero,) * 2, (zero,) * 2)
            carry = lax.fori_loop(1, slices - 1, slab, carry, unroll=True)
            _, middle, logs, _, white, tinted = carry
            logs = tuple(absorb(middle, side, logs[side])[0] for side in range(2))
        put = pl.ds(pl.multiple_of(start, 8), ROWS)
        for side in range(2):
            columns = pl.ds(side * LANES, LANES)
            res[step, 0, put, columns] = white[side]
            res[step, 1, put, columns] = tinted[side]
            res[step, 2, put, columns] = logs[side]

    def add_ends(tile, start, step):
        here, above, below = around(start)
        put = pl.ds(pl.multiple_of(start, 8), ROWS)
        first, last = outside(tile, start)
        for z in (0, slices - 1):
            ahead, middle, behind = (
                tuple(vol[tile + 1 + side, z + shift, here, :] for side in range(2))
                for shift in range(3)
            )
            ahead, behind = (first(), behind) if z == 0 else (ahead, last())
            for side in range(2):
                columns = pl.ds(side * LANES, LANES)
                value = middle[side]
                lambert = shade(tile, z, here, above, below, ahead[side], middle, behind[side], side)
                own = jnp.log2(1.0 + jnp.exp2(value * LOG2E))
                if z == 0:
                    passed = 1.0 - jnp.exp2(own * -density)
                else:
                    log = res[step, 2, put, columns]
                    passed = jnp.exp2((log + own) * density) - jnp.exp2(log * density)
                lit = passed * (lambert + lift)
                res[step, 0, put, columns] += lit
                res[step, 1, put, columns] += lit * jnp.tanh(value)

    def to_sibling(phase):
        return pltpu.make_async_remote_copy(
            src_ref=res.at[2 * phase],
            dst_ref=sib.at[phase],
            send_sem=sib_send.at[phase],
            recv_sem=sib_recv.at[phase],
            device_id={"depth": sibling},
            device_id_type=MESH,
        )

    pieces = ((2, ROWS, 2 * ROWS), (3, 0, ROWS), (4, 3 * ROWS, ROWS))

    def to_owner(phase, number, low, count):
        span = pl.ds(low, count)
        return pltpu.make_async_remote_copy(
            src_ref=res.at[2 * phase + 1, :, span, :],
            dst_ref=parts.at[phase, :, span, :],
            send_sem=part_send.at[number],
            recv_sem=part_recv.at[number],
            device_id={"depth": 2 * ((chip + ahead_of(phase)) % 4) + core},
            device_id_type=MESH,
        )

    def join(phase, chunks):
        for chunk in chunks:
            at = pl.ds(pl.multiple_of(chunk * ROWS, ROWS), ROWS)
            mine = [res[2 * phase + 1, plane, at, :] for plane in range(3)]
            other = [sib[phase, plane, at, :] for plane in range(3)]
            front = [jnp.where(core == 0, a, b) for a, b in zip(mine, other)]
            back = [jnp.where(core == 0, b, a) for a, b in zip(mine, other)]
            through = jnp.exp2(front[2] * density)
            res[2 * phase + 1, 0, at, :] = front[0] + through * back[0]
            res[2 * phase + 1, 1, at, :] = front[1] + through * back[1]
            res[2 * phase + 1, 2, at, :] = front[2] + back[2]

    def wait_loads(step):
        @pl.when(step == 0)
        def _():
            for position in order:
                load(position).wait()
            for position in range(11, 15):
                load(position).start()

        @pl.when(step == 1)
        def _():
            for position in range(5, 11):
                load(position).start()
            for position in second:
                load(position).wait()

        @pl.when(step == 2)
        def _():
            for position in range(11, 15):
                load(position).wait()

        @pl.when(step == 4)
        def _():
            for position in range(5, 11):
                load(position).wait()

    @pl.loop(0, EARLY)
    def _(step):
        wait_loads(step)

        @pl.when(step == 1)
        def _():
            pl.semaphore_wait(barrier, count)
            send_halos((0, 1, 2, 3), 0)
            send_halos((0, 1), 1)

        @pl.when(step == 2)
        def _():
            send_halos((2, 3), 1)
            send_halos((0, 1), 2)
            send_halos((0, 1), 3)

        @pl.when(step == 4)
        def _():
            send_halos((2, 3), 2)
            send_halos((2, 3), 3)

        block = block_of(depth, step)
        march(2 * block, ROWS, step, False)
        march(2 * block, 2 * ROWS, step, False)

    def finish(step, turn):
        phase, half = step // 2, step % 2
        early = step < EARLY
        pl.when((half == 0) & (turn == 1))(lambda: to_sibling(phase).start())

        @pl.when((half == 1) & (early | (turn == 0)))
        def _():
            to_sibling(phase).wait_recv()

        @pl.when((half == 1) & early)
        def _():
            join(phase, range(4))
            to_owner(phase, phase, 0, height).start()

        @pl.when((half == 1) & (step >= EARLY))
        def _():
            join(phase, (1 - turn, 2 + turn))

        @pl.when((step == 5) & (turn == 0))
        def _():
            to_owner(2, *pieces[0]).start()

        @pl.when((step == 5) & (turn == 1))
        def _():
            to_owner(2, *pieces[1]).start()
            to_owner(2, *pieces[2]).start()

    @pl.loop(0, EARLY)
    def _(step):
        pl.when(step % 2 == 0)(lambda: receive_halos((0, 1, 2, 3), step // 2))
        block = block_of(depth, step)
        add_ends(2 * block, ROWS, step)
        add_ends(2 * block, 2 * ROWS, step)
        march(2 * block, 0, step, True)
        march(2 * block, 3 * ROWS, step, True)
        finish(step, 1)

    @pl.loop(0, 2 * (8 - EARLY))
    def _(index):
        step, turn = EARLY + index // 2, index % 2
        pl.when((step % 2 == 0) & (turn == 0))(lambda: receive_halos((0, 1, 2, 3), step // 2))
        block = block_of(depth, step)
        march(2 * block, ROWS * (1 - turn), step, True)
        march(2 * block, ROWS * (2 + turn), step, True)
        finish(step, turn)

    sends = ((0, 0, 0, height), (1, 1, 0, height)) + tuple((2,) + piece for piece in pieces)
    for send in sends:
        to_owner(*send).wait_recv()

    scale = (1.0 - ambient) / 3.0
    slope = [scale * 0.5 * transfer[3 + colour] for colour in range(3)]
    base = [scale * transfer[colour] + slope[colour] for colour in range(3)]

    @pl.loop(0, height // ROWS, unroll=True)
    def _(chunk):
        at = pl.ds(pl.multiple_of(chunk * ROWS, ROWS), ROWS)
        white = tinted = log = jnp.zeros((ROWS, 2 * LANES), jnp.float32)
        for front in range(4):
            ahead = (chip + 4 - front) % 4
            own = ahead == 0
            slot = jnp.where(ahead == 2, 0, jnp.where(ahead == 3, 2, 1))
            part = [
                jnp.where(own, res[7, plane, at, :], parts[slot, plane, at, :])
                for plane in range(3)
            ]
            through = jnp.exp2(log * density)
            white = white + through * part[0]
            tinted = tinted + through * part[1]
            log = log + part[2]
        for colour in range(3):
            image[colour, at, :] = base[colour] * white + slope[colour] * tinted
        bend = jnp.tanh(log * (density * (-0.5 * LN2)))
        image[3, at, :] = 2.0 * bend / (1.0 + bend)

    for phase in range(4):
        to_sibling(phase).wait_send()
    for send in sends:
        to_owner(*send).wait_send()
    for kind in range(4):

        @pl.when(can_send[kind])
        def _(kind=kind):
            sent = slabs.at[0] if kind < 2 else vol.at[pl.ds(1, 16), pl.ds(1, slices), pl.ds(TOP, 1), :]
            pltpu.make_async_copy(sent, sent, halo_send.at[kind]).wait()


def on_device(volume, transfer):
    slices, height, columns = volume.shape
    own = columns // lax.axis_size("depth")
    f32 = jnp.float32
    dma = pltpu.SemaphoreType.DMA
    return pl.pallas_call(
        kernel,
        out_shape=pltpu.VMEM((4, height, own), f32),
        in_specs=[
            pl.BlockSpec(memory_space=pltpu.SMEM),
            pl.BlockSpec(memory_space=pl.ANY),
        ],
        out_specs=pl.BlockSpec(memory_space=pltpu.VMEM),
        scratch_shapes=[
            pltpu.VMEM((18, slices + 2, height + 16, LANES), f32),
            pltpu.VMEM((2, height, columns), f32),
            pltpu.VMEM((8, 3, height, own), f32),
            pltpu.VMEM((4, 3, height, own), f32),
            pltpu.VMEM((3, 3, height, own), f32),
            dma((16,)),
            dma((4,)),
            dma((4, 4)),
            dma((4,)),
            dma((4,)),
            dma((5,)),
            dma((5,)),
        ],
        compiler_params=pltpu.CompilerParams(
            collective_id=0, has_side_effects=True, vmem_limit_bytes=56 * 1024 * 1024
        ),
        name="render",
    )(transfer, volume)


def solution(mesh):
    in_specs = (P("depth", "row", None), P())
    out_specs = P(None, "row", "depth")
    return jax.shard_map(
        on_device, mesh=mesh, in_specs=in_specs, out_specs=out_specs, check_vma=False
    )
```

```python
import jax
import jax.numpy as jnp
from jax import lax
from jax.experimental import pallas as pl
from jax.experimental.pallas import tpu as pltpu
from jax.sharding import PartitionSpec as P

LOG2E = 1.4426950408889634
LN2 = 0.6931471805599453
LANES = 128
ROWS = 16
TOP = 8
EARLY = 5
MESH = pl.DeviceIdType.MESH


def ahead_of(phase):
    return jnp.where(phase == 0, 2, jnp.where(phase == 1, 1, jnp.where(phase == 2, 3, 0)))


def block_of(depth, step):
    chip, core = depth // 2, depth % 2
    phase, half = step // 2, step % 2
    parity = core * half + (1 - core) * (1 - half)
    return 2 * ((chip + ahead_of(phase)) % 4) + parity


def kernel(
    transfer,
    volume,
    image,
    vol,
    slabs,
    res,
    sib,
    parts,
    load_sem,
    halo_send,
    halo_recv,
    sib_send,
    sib_recv,
    part_send,
    part_recv,
):
    depth, row = lax.axis_index("depth"), lax.axis_index("row")
    depths, rows = lax.axis_size("depth"), lax.axis_size("row")
    slices, height, _ = volume.shape
    chip, core = depth // 2, depth % 2
    sibling = depth + 1 - 2 * core
    first = 4 * ((chip + 2) % 4)

    def load(position):
        tile = (first + position) % 16
        return pltpu.make_async_copy(
            volume.at[:, :, pl.ds(pl.multiple_of(tile * LANES, LANES), LANES)],
            vol.at[tile + 1, pl.ds(1, slices), pl.ds(TOP, height), :],
            load_sem.at[tile],
        )

    lead = 2 - 2 * core
    order = [lead + 15, lead, lead + 1, lead + 2]
    second = [3 * core, 15 + 5 * core]

    def partners(act):
        for offset in (2, 4, 6):
            act(True, {"depth": (depth + offset) % depths})
        act(depth > 0, {"depth": depth - 1})
        act(depth < depths - 1, {"depth": depth + 1})
        act(row > 0, {"row": row - 1})
        act(row < rows - 1, {"row": row + 1})

    barrier = pltpu.get_barrier_semaphore()

    def greet(there, device):
        def signal():
            pl.semaphore_signal(barrier, inc=1, device_id=device, device_id_type=MESH)

        signal() if there is True else pl.when(there)(signal)

    partners(greet)
    for position in order + second + list(range(11, 15)):
        load(position).start()

    @pl.loop(0, slices)
    def _(z):
        vol[0, z + 1, pl.ds(TOP, height), :] = jnp.zeros((height, LANES), jnp.float32)
        vol[17, z + 1, pl.ds(TOP, height), :] = jnp.zeros((height, LANES), jnp.float32)

    def clear_slab(kind):
        slabs[kind] = jnp.zeros((height, 16 * LANES), jnp.float32)

    def clear_row(at):
        @pl.loop(0, 16)
        def _(tile):
            for z in range(slices):
                vol[tile + 1, z + 1, pl.ds(at, 1), :] = jnp.zeros((1, LANES), jnp.float32)

    pl.when(depth == 0)(lambda: clear_slab(0))
    pl.when(depth == depths - 1)(lambda: clear_slab(1))
    pl.when(row == 0)(lambda: clear_row(TOP - 1))
    pl.when(row == rows - 1)(lambda: clear_row(TOP + height))

    count = 3 + (depth > 0).astype(jnp.int32) + (depth < depths - 1).astype(jnp.int32)
    count = count + (row > 0).astype(jnp.int32) + (row < rows - 1).astype(jnp.int32)

    def halo(kind, group):
        if kind < 2:
            columns = pl.ds(pl.multiple_of(group * 4 * LANES, 4 * LANES), 4 * LANES)
            source = volume.at[slices - 1 if kind == 0 else 0, :, columns]
            target = slabs.at[kind, :, columns]
            device = {"depth": depth + 1 if kind == 0 else depth - 1}
        else:
            tiles = pl.ds(4 * group + 1, 4)
            last, beyond = (TOP + height - 1, TOP - 1) if kind == 2 else (TOP, TOP + height)
            source = vol.at[tiles, pl.ds(1, slices), pl.ds(last, 1), :]
            target = vol.at[tiles, pl.ds(1, slices), pl.ds(beyond, 1), :]
            device = {"row": row + 1 if kind == 2 else row - 1}
        return pltpu.make_async_remote_copy(
            src_ref=source,
            dst_ref=target,
            send_sem=halo_send.at[kind],
            recv_sem=halo_recv.at[kind, group],
            device_id=device,
            device_id_type=MESH,
        )

    can_send = (depth < depths - 1, depth > 0, row < rows - 1, row > 0)
    can_receive = (depth > 0, depth < depths - 1, row > 0, row < rows - 1)

    def group_of(depth, phase):
        return (depth // 2 + ahead_of(phase)) % 4

    def send_halos(kinds, phase):
        for kind in kinds:

            @pl.when(can_send[kind])
            def _(kind=kind):
                halo(kind, group_of((depth + 1, depth - 1, depth, depth)[kind], phase)).start()

    def receive_halos(kinds, phase):
        for kind in kinds:

            @pl.when(can_receive[kind])
            def _(kind=kind):
                halo(kind, group_of(depth, phase)).wait_recv()

    density = transfer[6] * (2.0 / (slices * depths))
    ambient = 0.5 * transfer[7]
    lift = 3.0 * ambient / (1.0 - ambient)
    lane = lax.broadcasted_iota(jnp.int32, (ROWS, LANES), 1)
    lowest, highest = lane == 0, lane == LANES - 1

    def shade(tile, z, here, above, below, ahead, middle, behind, side):
        value = middle[side]
        if side == 0:
            before, after = vol[tile, z + 1, here, :], middle[1]
        else:
            before, after = middle[0], vol[tile + 3, z + 1, here, :]
        left = pltpu.roll(jnp.where(highest, before, value), 1, 1)
        right = pltpu.roll(jnp.where(lowest, after, value), LANES - 1, 1)
        by_depth = behind - ahead
        by_row = vol[tile + 1 + side, z + 1, below, :] - vol[tile + 1 + side, z + 1, above, :]
        by_column = right - left
        plane = by_row + by_column
        along = by_depth + (plane + plane)
        square = (by_depth * by_depth + 4.0) + (by_row * by_row + by_column * by_column)
        return jnp.abs(along) * lax.rsqrt(square)

    def around(start):
        return tuple(pl.ds(TOP + start + shift, ROWS) for shift in (0, -1, 1))

    def outside(tile, start):
        put = pl.ds(pl.multiple_of(start, 8), ROWS)
        columns = [pl.ds(pl.multiple_of((tile + side) * LANES, LANES), LANES) for side in range(2)]
        return [lambda kind=kind: tuple(slabs[kind, put, column] for column in columns) for kind in range(2)]

    def march(tile, start, step, ends):
        here, above, below = around(start)

        def cells(slab):
            return tuple(vol[tile + 1 + side, slab, here, :] for side in range(2))

        first, last = outside(tile, start)

        def absorb(middle, side, log):
            log = log - jnp.log2(1.0 + jnp.exp2(middle[side] * LOG2E))
            return log, jnp.exp2(log * density)

        def slab(z, carry, behind=None):
            ahead, middle, logs, passing, white, tinted = carry
            behind = cells(z + 2) if behind is None else behind
            out = []
            for side in range(2):
                lambert = shade(tile, z, here, above, below, ahead[side], middle, behind[side], side)
                log, after = absorb(middle, side, logs[side])
                lit = (passing[side] - after) * (lambert + lift)
                tint = jnp.tanh(middle[side])
                out.append((log, after, white[side] + lit, tinted[side] + lit * tint))
            return (middle, behind) + tuple(zip(*out))

        zero = jnp.zeros((ROWS, LANES), jnp.float32)
        if ends:
            carry = (first(), cells(1), (zero,) * 2, (zero + 1.0,) * 2, (zero,) * 2, (zero,) * 2)
            carry = lax.fori_loop(0, slices - 1, slab, carry, unroll=True)
            _, _, logs, _, white, tinted = slab(slices - 1, carry, last())
        else:
            middle = cells(1)
            logs, passing = zip(*(absorb(middle, side, zero) for side in range(2)))
            carry = (middle, cells(2), logs, passing, (zero,) * 2, (zero,) * 2)
            carry = lax.fori_loop(1, slices - 1, slab, carry, unroll=True)
            _, middle, logs, _, white, tinted = carry
            logs = tuple(absorb(middle, side, logs[side])[0] for side in range(2))
        put = pl.ds(pl.multiple_of(start, 8), ROWS)
        for side in range(2):
            columns = pl.ds(side * LANES, LANES)
            res[step, 0, put, columns] = white[side]
            res[step, 1, put, columns] = tinted[side]
            res[step, 2, put, columns] = logs[side]

    def add_ends(tile, start, step):
        here, above, below = around(start)
        put = pl.ds(pl.multiple_of(start, 8), ROWS)
        first, last = outside(tile, start)
        for z in (0, slices - 1):
            ahead, middle, behind = (
                tuple(vol[tile + 1 + side, z + shift, here, :] for side in range(2))
                for shift in range(3)
            )
            ahead, behind = (first(), behind) if z == 0 else (ahead, last())
            for side in range(2):
                columns = pl.ds(side * LANES, LANES)
                value = middle[side]
                lambert = shade(tile, z, here, above, below, ahead[side], middle, behind[side], side)
                own = jnp.log2(1.0 + jnp.exp2(value * LOG2E))
                if z == 0:
                    passed = 1.0 - jnp.exp2(own * -density)
                else:
                    log = res[step, 2, put, columns]
                    passed = jnp.exp2((log + own) * density) - jnp.exp2(log * density)
                lit = passed * (lambert + lift)
                res[step, 0, put, columns] += lit
                res[step, 1, put, columns] += lit * jnp.tanh(value)

    def to_sibling(phase):
        return pltpu.make_async_remote_copy(
            src_ref=res.at[2 * phase],
            dst_ref=sib.at[phase],
            send_sem=sib_send.at[phase],
            recv_sem=sib_recv.at[phase],
            device_id={"depth": sibling},
            device_id_type=MESH,
        )

    pieces = ((2, ROWS, 2 * ROWS), (3, 0, ROWS), (4, 3 * ROWS, ROWS))

    def to_owner(phase, number, low, count):
        span = pl.ds(low, count)
        return pltpu.make_async_remote_copy(
            src_ref=res.at[2 * phase + 1, :, span, :],
            dst_ref=parts.at[phase, :, span, :],
            send_sem=part_send.at[number],
            recv_sem=part_recv.at[number],
            device_id={"depth": 2 * ((chip + ahead_of(phase)) % 4) + core},
            device_id_type=MESH,
        )

    def join(phase, chunks):
        for chunk in chunks:
            at = pl.ds(pl.multiple_of(chunk * ROWS, ROWS), ROWS)
            mine = [res[2 * phase + 1, plane, at, :] for plane in range(3)]
            other = [sib[phase, plane, at, :] for plane in range(3)]
            front = [jnp.where(core == 0, a, b) for a, b in zip(mine, other)]
            back = [jnp.where(core == 0, b, a) for a, b in zip(mine, other)]
            through = jnp.exp2(front[2] * density)
            res[2 * phase + 1, 0, at, :] = front[0] + through * back[0]
            res[2 * phase + 1, 1, at, :] = front[1] + through * back[1]
            res[2 * phase + 1, 2, at, :] = front[2] + back[2]

    def wait_loads(step):
        @pl.when(step == 0)
        def _():
            for position in order:
                load(position).wait()

        @pl.when(step == 1)
        def _():
            for position in range(5, 11):
                load(position).start()
            for position in second:
                load(position).wait()

        @pl.when(step == 2)
        def _():
            for position in range(11, 15):
                load(position).wait()

        @pl.when(step == 4)
        def _():
            for position in range(5, 11):
                load(position).wait()

    @pl.loop(0, EARLY)
    def _(step):
        wait_loads(step)

        @pl.when(step == 1)
        def _():
            pl.semaphore_wait(barrier, count)
            send_halos((0, 1, 2, 3), 0)
            send_halos((0, 1), 1)

        @pl.when(step == 2)
        def _():
            send_halos((2, 3), 1)
            send_halos((0, 1), 2)
            send_halos((0, 1), 3)

        @pl.when(step == 4)
        def _():
            send_halos((2, 3), 2)
            send_halos((2, 3), 3)

        block = block_of(depth, step)
        march(2 * block, ROWS, step, False)
        march(2 * block, 2 * ROWS, step, False)

    def finish(step, turn):
        phase, half = step // 2, step % 2
        early = step < EARLY
        pl.when((half == 0) & (turn == 1))(lambda: to_sibling(phase).start())

        @pl.when((half == 1) & (early | (turn == 0)))
        def _():
            to_sibling(phase).wait_recv()

        @pl.when((half == 1) & early)
        def _():
            join(phase, range(4))
            to_owner(phase, phase, 0, height).start()

        @pl.when((half == 1) & (step >= EARLY))
        def _():
            join(phase, (1 - turn, 2 + turn))

        @pl.when((step == 5) & (turn == 0))
        def _():
            to_owner(2, *pieces[0]).start()

        @pl.when((step == 5) & (turn == 1))
        def _():
            to_owner(2, *pieces[1]).start()
            to_owner(2, *pieces[2]).start()

    @pl.loop(0, EARLY)
    def _(step):
        pl.when(step % 2 == 0)(lambda: receive_halos((0, 1, 2, 3), step // 2))
        block = block_of(depth, step)
        add_ends(2 * block, ROWS, step)
        add_ends(2 * block, 2 * ROWS, step)
        march(2 * block, 0, step, True)
        march(2 * block, 3 * ROWS, step, True)
        finish(step, 1)

    @pl.loop(0, 2 * (8 - EARLY))
    def _(index):
        step, turn = EARLY + index // 2, index % 2
        pl.when((step % 2 == 0) & (turn == 0))(lambda: receive_halos((0, 1, 2, 3), step // 2))
        block = block_of(depth, step)
        march(2 * block, ROWS * (1 - turn), step, True)
        march(2 * block, ROWS * (2 + turn), step, True)
        finish(step, turn)

    sends = ((0, 0, 0, height), (1, 1, 0, height)) + tuple((2,) + piece for piece in pieces)
    for send in sends:
        to_owner(*send).wait_recv()

    scale = (1.0 - ambient) / 3.0
    slope = [scale * 0.5 * transfer[3 + colour] for colour in range(3)]
    base = [scale * transfer[colour] + slope[colour] for colour in range(3)]

    @pl.loop(0, height // ROWS, unroll=True)
    def _(chunk):
        at = pl.ds(pl.multiple_of(chunk * ROWS, ROWS), ROWS)
        white = tinted = log = jnp.zeros((ROWS, 2 * LANES), jnp.float32)
        for front in range(4):
            ahead = (chip + 4 - front) % 4
            own = ahead == 0
            slot = jnp.where(ahead == 2, 0, jnp.where(ahead == 3, 2, 1))
            part = [
                jnp.where(own, res[7, plane, at, :], parts[slot, plane, at, :])
                for plane in range(3)
            ]
            through = jnp.exp2(log * density)
            white = white + through * part[0]
            tinted = tinted + through * part[1]
            log = log + part[2]
        for colour in range(3):
            image[colour, at, :] = base[colour] * white + slope[colour] * tinted
        bend = jnp.tanh(log * (density * (-0.5 * LN2)))
        image[3, at, :] = 2.0 * bend / (1.0 + bend)

    for phase in range(4):
        to_sibling(phase).wait_send()
    for send in sends:
        to_owner(*send).wait_send()
    for kind in range(4):

        @pl.when(can_send[kind])
        def _(kind=kind):
            sent = slabs.at[0] if kind < 2 else vol.at[pl.ds(1, 16), pl.ds(1, slices), pl.ds(TOP, 1), :]
            pltpu.make_async_copy(sent, sent, halo_send.at[kind]).wait()


def on_device(volume, transfer):
    slices, height, columns = volume.shape
    own = columns // lax.axis_size("depth")
    f32 = jnp.float32
    dma = pltpu.SemaphoreType.DMA
    return pl.pallas_call(
        kernel,
        out_shape=pltpu.VMEM((4, height, own), f32),
        in_specs=[
            pl.BlockSpec(memory_space=pltpu.SMEM),
            pl.BlockSpec(memory_space=pl.ANY),
        ],
        out_specs=pl.BlockSpec(memory_space=pltpu.VMEM),
        scratch_shapes=[
            pltpu.VMEM((18, slices + 2, height + 16, LANES), f32),
            pltpu.VMEM((2, height, columns), f32),
            pltpu.VMEM((8, 3, height, own), f32),
            pltpu.VMEM((4, 3, height, own), f32),
            pltpu.VMEM((3, 3, height, own), f32),
            dma((16,)),
            dma((4,)),
            dma((4, 4)),
            dma((4,)),
            dma((4,)),
            dma((5,)),
            dma((5,)),
        ],
        compiler_params=pltpu.CompilerParams(
            collective_id=0, has_side_effects=True, vmem_limit_bytes=56 * 1024 * 1024
        ),
        name="render",
    )(transfer, volume)


def solution(mesh):
    in_specs = (P("depth", "row", None), P())
    out_specs = P(None, "row", "depth")
    return jax.shard_map(
        on_device, mesh=mesh, in_specs=in_specs, out_specs=out_specs, check_vma=False
    )
```

```python
import jax
import jax.numpy as jnp
from jax import lax
from jax.experimental import pallas as pl
from jax.experimental.pallas import tpu as pltpu
from jax.sharding import PartitionSpec as P

LOG2E = 1.4426950408889634
LN2 = 0.6931471805599453
LANES = 128
ROWS = 16
TOP = 8
EARLY = 5
MESH = pl.DeviceIdType.MESH


def ahead_of(phase):
    return jnp.where(phase == 0, 2, jnp.where(phase == 1, 1, jnp.where(phase == 2, 3, 0)))


def block_of(depth, step):
    chip, core = depth // 2, depth % 2
    phase, half = step // 2, step % 2
    parity = core * half + (1 - core) * (1 - half)
    return 2 * ((chip + ahead_of(phase)) % 4) + parity


def kernel(
    transfer,
    volume,
    image,
    vol,
    slabs,
    res,
    sib,
    parts,
    load_sem,
    halo_send,
    halo_recv,
    sib_send,
    sib_recv,
    part_send,
    part_recv,
):
    depth, row = lax.axis_index("depth"), lax.axis_index("row")
    depths, rows = lax.axis_size("depth"), lax.axis_size("row")
    slices, height, _ = volume.shape
    chip, core = depth // 2, depth % 2
    sibling = depth + 1 - 2 * core
    first = 4 * ((chip + 2) % 4)

    def load(position):
        tile = (first + position) % 16
        return pltpu.make_async_copy(
            volume.at[:, :, pl.ds(pl.multiple_of(tile * LANES, LANES), LANES)],
            vol.at[tile + 1, pl.ds(1, slices), pl.ds(TOP, height), :],
            load_sem.at[tile],
        )

    lead = 2 - 2 * core
    order = [lead + 15, lead, lead + 1, lead + 2]
    second = [3 * core, 15 + 5 * core]

    def partners(act):
        for offset in (2, 4, 6):
            act(True, {"depth": (depth + offset) % depths})
        act(depth > 0, {"depth": depth - 1})
        act(depth < depths - 1, {"depth": depth + 1})
        act(row > 0, {"row": row - 1})
        act(row < rows - 1, {"row": row + 1})

    barrier = pltpu.get_barrier_semaphore()

    def greet(there, device):
        def signal():
            pl.semaphore_signal(barrier, inc=1, device_id=device, device_id_type=MESH)

        signal() if there is True else pl.when(there)(signal)

    partners(greet)
    for position in order + second + list(range(11, 15)):
        load(position).start()

    @pl.loop(0, slices)
    def _(z):
        vol[0, z + 1, pl.ds(TOP, height), :] = jnp.zeros((height, LANES), jnp.float32)
        vol[17, z + 1, pl.ds(TOP, height), :] = jnp.zeros((height, LANES), jnp.float32)

    def clear_slab(kind):
        slabs[kind] = jnp.zeros((height, 16 * LANES), jnp.float32)

    def clear_row(at):
        @pl.loop(0, 16)
        def _(tile):
            for z in range(slices):
                vol[tile + 1, z + 1, pl.ds(at, 1), :] = jnp.zeros((1, LANES), jnp.float32)

    pl.when(depth == 0)(lambda: clear_slab(0))
    pl.when(depth == depths - 1)(lambda: clear_slab(1))
    pl.when(row == 0)(lambda: clear_row(TOP - 1))
    pl.when(row == rows - 1)(lambda: clear_row(TOP + height))

    count = 3 + (depth > 0).astype(jnp.int32) + (depth < depths - 1).astype(jnp.int32)
    count = count + (row > 0).astype(jnp.int32) + (row < rows - 1).astype(jnp.int32)

    def halo(kind, group):
        if kind < 2:
            columns = pl.ds(pl.multiple_of(group * 4 * LANES, 4 * LANES), 4 * LANES)
            source = volume.at[slices - 1 if kind == 0 else 0, :, columns]
            target = slabs.at[kind, :, columns]
            device = {"depth": depth + 1 if kind == 0 else depth - 1}
        else:
            tiles = pl.ds(4 * group + 1, 4)
            last, beyond = (TOP + height - 1, TOP - 1) if kind == 2 else (TOP, TOP + height)
            source = vol.at[tiles, pl.ds(1, slices), pl.ds(last, 1), :]
            target = vol.at[tiles, pl.ds(1, slices), pl.ds(beyond, 1), :]
            device = {"row": row + 1 if kind == 2 else row - 1}
        return pltpu.make_async_remote_copy(
            src_ref=source,
            dst_ref=target,
            send_sem=halo_send.at[kind],
            recv_sem=halo_recv.at[kind, group],
            device_id=device,
            device_id_type=MESH,
        )

    can_send = (depth < depths - 1, depth > 0, row < rows - 1, row > 0)
    can_receive = (depth > 0, depth < depths - 1, row > 0, row < rows - 1)

    def group_of(depth, phase):
        return (depth // 2 + ahead_of(phase)) % 4

    def send_halos(kinds, phase):
        for kind in kinds:

            @pl.when(can_send[kind])
            def _(kind=kind):
                halo(kind, group_of((depth + 1, depth - 1, depth, depth)[kind], phase)).start()

    def receive_halos(kinds, phase):
        for kind in kinds:

            @pl.when(can_receive[kind])
            def _(kind=kind):
                halo(kind, group_of(depth, phase)).wait_recv()

    density = transfer[6] * (2.0 / (slices * depths))
    ambient = 0.5 * transfer[7]
    lift = 3.0 * ambient / (1.0 - ambient)
    lane = lax.broadcasted_iota(jnp.int32, (ROWS, LANES), 1)
    lowest, highest = lane == 0, lane == LANES - 1

    def shade(tile, z, here, above, below, ahead, middle, behind, side):
        value = middle[side]
        if side == 0:
            before, after = vol[tile, z + 1, here, :], middle[1]
        else:
            before, after = middle[0], vol[tile + 3, z + 1, here, :]
        left = pltpu.roll(jnp.where(highest, before, value), 1, 1)
        right = pltpu.roll(jnp.where(lowest, after, value), LANES - 1, 1)
        by_depth = behind - ahead
        by_row = vol[tile + 1 + side, z + 1, below, :] - vol[tile + 1 + side, z + 1, above, :]
        by_column = right - left
        plane = by_row + by_column
        along = by_depth + (plane + plane)
        square = (by_depth * by_depth + 4.0) + (by_row * by_row + by_column * by_column)
        return jnp.abs(along) * lax.rsqrt(square)

    def around(start):
        return tuple(pl.ds(TOP + start + shift, ROWS) for shift in (0, -1, 1))

    def outside(tile, start):
        put = pl.ds(pl.multiple_of(start, 8), ROWS)
        columns = [pl.ds(pl.multiple_of((tile + side) * LANES, LANES), LANES) for side in range(2)]
        return [lambda kind=kind: tuple(slabs[kind, put, column] for column in columns) for kind in range(2)]

    def march(tile, start, step, ends):
        here, above, below = around(start)

        def cells(slab):
            return tuple(vol[tile + 1 + side, slab, here, :] for side in range(2))

        first, last = outside(tile, start)

        def absorb(middle, side, log):
            log = log - jnp.log2(1.0 + jnp.exp2(middle[side] * LOG2E))
            return log, jnp.exp2(log * density)

        def slab(z, carry, behind=None):
            ahead, middle, logs, passing, white, tinted = carry
            behind = cells(z + 2) if behind is None else behind
            out = []
            for side in range(2):
                lambert = shade(tile, z, here, above, below, ahead[side], middle, behind[side], side)
                log, after = absorb(middle, side, logs[side])
                lit = (passing[side] - after) * (lambert + lift)
                tint = jnp.tanh(middle[side])
                out.append((log, after, white[side] + lit, tinted[side] + lit * tint))
            return (middle, behind) + tuple(zip(*out))

        zero = jnp.zeros((ROWS, LANES), jnp.float32)
        if ends:
            carry = (first(), cells(1), (zero,) * 2, (zero + 1.0,) * 2, (zero,) * 2, (zero,) * 2)
            carry = lax.fori_loop(0, slices - 1, slab, carry, unroll=True)
            _, _, logs, _, white, tinted = slab(slices - 1, carry, last())
        else:
            middle = cells(1)
            logs, passing = zip(*(absorb(middle, side, zero) for side in range(2)))
            carry = (middle, cells(2), logs, passing, (zero,) * 2, (zero,) * 2)
            carry = lax.fori_loop(1, slices - 1, slab, carry, unroll=True)
            _, middle, logs, _, white, tinted = carry
            logs = tuple(absorb(middle, side, logs[side])[0] for side in range(2))
        put = pl.ds(pl.multiple_of(start, 8), ROWS)
        for side in range(2):
            columns = pl.ds(side * LANES, LANES)
            res[step, 0, put, columns] = white[side]
            res[step, 1, put, columns] = tinted[side]
            res[step, 2, put, columns] = logs[side]

    def add_ends(tile, start, step):
        here, above, below = around(start)
        put = pl.ds(pl.multiple_of(start, 8), ROWS)
        first, last = outside(tile, start)
        for z in (0, slices - 1):
            ahead, middle, behind = (
                tuple(vol[tile + 1 + side, z + shift, here, :] for side in range(2))
                for shift in range(3)
            )
            ahead, behind = (first(), behind) if z == 0 else (ahead, last())
            for side in range(2):
                columns = pl.ds(side * LANES, LANES)
                value = middle[side]
                lambert = shade(tile, z, here, above, below, ahead[side], middle, behind[side], side)
                own = jnp.log2(1.0 + jnp.exp2(value * LOG2E))
                if z == 0:
                    passed = 1.0 - jnp.exp2(own * -density)
                else:
                    log = res[step, 2, put, columns]
                    passed = jnp.exp2((log + own) * density) - jnp.exp2(log * density)
                lit = passed * (lambert + lift)
                res[step, 0, put, columns] += lit
                res[step, 1, put, columns] += lit * jnp.tanh(value)

    def to_sibling(phase):
        return pltpu.make_async_remote_copy(
            src_ref=res.at[2 * phase],
            dst_ref=sib.at[phase],
            send_sem=sib_send.at[phase],
            recv_sem=sib_recv.at[phase],
            device_id={"depth": sibling},
            device_id_type=MESH,
        )

    pieces = ((2, ROWS, 2 * ROWS), (3, 0, ROWS), (4, 3 * ROWS, ROWS))

    def to_owner(phase, number, low, count):
        span = pl.ds(low, count)
        return pltpu.make_async_remote_copy(
            src_ref=res.at[2 * phase + 1, :, span, :],
            dst_ref=parts.at[phase, :, span, :],
            send_sem=part_send.at[number],
            recv_sem=part_recv.at[number],
            device_id={"depth": 2 * ((chip + ahead_of(phase)) % 4) + core},
            device_id_type=MESH,
        )

    def join(phase, chunks):
        for chunk in chunks:
            at = pl.ds(pl.multiple_of(chunk * ROWS, ROWS), ROWS)
            mine = [res[2 * phase + 1, plane, at, :] for plane in range(3)]
            other = [sib[phase, plane, at, :] for plane in range(3)]
            front = [jnp.where(core == 0, a, b) for a, b in zip(mine, other)]
            back = [jnp.where(core == 0, b, a) for a, b in zip(mine, other)]
            through = jnp.exp2(front[2] * density)
            res[2 * phase + 1, 0, at, :] = front[0] + through * back[0]
            res[2 * phase + 1, 1, at, :] = front[1] + through * back[1]
            res[2 * phase + 1, 2, at, :] = front[2] + back[2]

    def wait_loads(step):
        @pl.when(step == 0)
        def _():
            for position in order:
                load(position).wait()

        @pl.when(step == 1)
        def _():
            for position in range(5, 11):
                load(position).start()
            for position in second:
                load(position).wait()

        @pl.when(step == 2)
        def _():
            for position in range(11, 15):
                load(position).wait()

        @pl.when(step == 4)
        def _():
            for position in range(5, 11):
                load(position).wait()

    @pl.loop(0, EARLY)
    def _(step):
        @pl.when(step == 1)
        def _():
            pl.semaphore_wait(barrier, count)
            send_halos((0, 1), 0)

        wait_loads(step)

        @pl.when(step == 1)
        def _():
            send_halos((2, 3), 0)

        @pl.when(step == 2)
        def _():
            send_halos((0, 1, 2, 3), 1)

        @pl.when(step == 4)
        def _():
            send_halos((0, 1, 2, 3), 2)
            send_halos((0, 1, 2, 3), 3)

        block = block_of(depth, step)
        march(2 * block, ROWS, step, False)
        march(2 * block, 2 * ROWS, step, False)

    def finish(step, turn):
        phase, half = step // 2, step % 2
        early = step < EARLY
        pl.when((half == 0) & (turn == 1))(lambda: to_sibling(phase).start())

        @pl.when((half == 1) & (early | (turn == 0)))
        def _():
            to_sibling(phase).wait_recv()

        @pl.when((half == 1) & early)
        def _():
            join(phase, range(4))
            to_owner(phase, phase, 0, height).start()

        @pl.when((half == 1) & (step >= EARLY))
        def _():
            join(phase, (1 - turn, 2 + turn))

        @pl.when((step == 5) & (turn == 0))
        def _():
            to_owner(2, *pieces[0]).start()

        @pl.when((step == 5) & (turn == 1))
        def _():
            to_owner(2, *pieces[1]).start()
            to_owner(2, *pieces[2]).start()

    @pl.loop(0, EARLY)
    def _(step):
        pl.when(step % 2 == 0)(lambda: receive_halos((0, 1, 2, 3), step // 2))
        block = block_of(depth, step)
        add_ends(2 * block, ROWS, step)
        add_ends(2 * block, 2 * ROWS, step)
        march(2 * block, 0, step, True)
        march(2 * block, 3 * ROWS, step, True)
        finish(step, 1)

    @pl.loop(0, 2 * (8 - EARLY))
    def _(index):
        step, turn = EARLY + index // 2, index % 2
        pl.when((step % 2 == 0) & (turn == 0))(lambda: receive_halos((0, 1, 2, 3), step // 2))
        block = block_of(depth, step)
        march(2 * block, ROWS * (1 - turn), step, True)
        march(2 * block, ROWS * (2 + turn), step, True)
        finish(step, turn)

    sends = ((0, 0, 0, height), (1, 1, 0, height)) + tuple((2,) + piece for piece in pieces)
    for send in sends:
        to_owner(*send).wait_recv()

    scale = (1.0 - ambient) / 3.0
    slope = [scale * 0.5 * transfer[3 + colour] for colour in range(3)]
    base = [scale * transfer[colour] + slope[colour] for colour in range(3)]

    @pl.loop(0, height // ROWS, unroll=True)
    def _(chunk):
        at = pl.ds(pl.multiple_of(chunk * ROWS, ROWS), ROWS)
        white = tinted = log = jnp.zeros((ROWS, 2 * LANES), jnp.float32)
        for front in range(4):
            ahead = (chip + 4 - front) % 4
            own = ahead == 0
            slot = jnp.where(ahead == 2, 0, jnp.where(ahead == 3, 2, 1))
            part = [
                jnp.where(own, res[7, plane, at, :], parts[slot, plane, at, :])
                for plane in range(3)
            ]
            through = jnp.exp2(log * density)
            white = white + through * part[0]
            tinted = tinted + through * part[1]
            log = log + part[2]
        for colour in range(3):
            image[colour, at, :] = base[colour] * white + slope[colour] * tinted
        bend = jnp.tanh(log * (density * (-0.5 * LN2)))
        image[3, at, :] = 2.0 * bend / (1.0 + bend)

    for phase in range(4):
        to_sibling(phase).wait_send()
    for send in sends:
        to_owner(*send).wait_send()
    for kind in range(4):

        @pl.when(can_send[kind])
        def _(kind=kind):
            sent = slabs.at[0] if kind < 2 else vol.at[pl.ds(1, 16), pl.ds(1, slices), pl.ds(TOP, 1), :]
            pltpu.make_async_copy(sent, sent, halo_send.at[kind]).wait()


def on_device(volume, transfer):
    slices, height, columns = volume.shape
    own = columns // lax.axis_size("depth")
    f32 = jnp.float32
    dma = pltpu.SemaphoreType.DMA
    return pl.pallas_call(
        kernel,
        out_shape=pltpu.VMEM((4, height, own), f32),
        in_specs=[
            pl.BlockSpec(memory_space=pltpu.SMEM),
            pl.BlockSpec(memory_space=pl.ANY),
        ],
        out_specs=pl.BlockSpec(memory_space=pltpu.VMEM),
        scratch_shapes=[
            pltpu.VMEM((18, slices + 2, height + 16, LANES), f32),
            pltpu.VMEM((2, height, columns), f32),
            pltpu.VMEM((8, 3, height, own), f32),
            pltpu.VMEM((4, 3, height, own), f32),
            pltpu.VMEM((3, 3, height, own), f32),
            dma((16,)),
            dma((4,)),
            dma((4, 4)),
            dma((4,)),
            dma((4,)),
            dma((5,)),
            dma((5,)),
        ],
        compiler_params=pltpu.CompilerParams(
            collective_id=0, has_side_effects=True, vmem_limit_bytes=56 * 1024 * 1024
        ),
        name="render",
    )(transfer, volume)


def solution(mesh):
    in_specs = (P("depth", "row", None), P())
    out_specs = P(None, "row", "depth")
    return jax.shard_map(
        on_device, mesh=mesh, in_specs=in_specs, out_specs=out_specs, check_vma=False
    )
```
